32 devices in a mesh: obs: 1, det: 32 (over z, y, x, core), tm: 1.
Axes of the slice: x: 2, y: 2, z: 4, core: 2. Of those that a mesh axis runs over, the one named last changes fastest.
Arguments:
- timestreams: float32 [2048, 512], P(('obs', 'det'), 'tm'), may hold values from -12 to 12
- pointing: int32 [2048, 512], P(('obs', 'det'), 'tm'), may hold values from 0 to 4095, as said below
- det_flags: int32 [2048], P(('obs', 'det')), may hold values 0 or 1
- det_weight: float32 [2048], P(('obs', 'det')), may hold values from 0.2 to 2
- block_slot: int32 [32], replicated, may hold values from 0 to 31, each once
- start_modes: float32 [512, 64], P('tm'), may hold values from -6 to 6
Outputs:
- modes: float32 [512, 64], P(('obs', 'tm'))
- signal_map: float32 [32, 128], P(('obs', 'det'))
- weight_map: float32 [32, 128], P(('obs', 'det'))
The draws below stay inside these ranges and needn't reach their ends.
Inputs may be any that keep to these rules, and one draw needn't show every extreme that they name: `pointing`: every sample of a detector in the aligned group g of 64 detector rows lies in a pixel block (g + r) mod 32 for some r from 0 to 3.
All inputs are finite; a program needn't handle non-finite values. No bound on the sum of `det_flags` on one device may be relied on, other than what follows from the above.
Results may differ from the reference program's by a relative error of at most 0.0029.
Values sent between devices are 32-bit elements; how exact they have to be, the bound alone decides.
A program may use at most 64 MiB of HBM per device.

```python
import math
import jax
import jax.numpy as jnp
from jax import lax

DET_DEV = 64
K = 64
ITERS = 2
PB = 128
DETS = 2048
NT = 512
NBLK = 32


def draw_timestreams(key, part):
    keys = jax.random.split(jax.random.fold_in(key, 101), 4)
    white_noise = jax.random.normal(keys[0], (DETS, NT), jnp.float32)
    mixing = jax.random.normal(keys[1], (DETS, K), jnp.float32)
    mode_rows = jax.random.normal(keys[2], (K, NT), jnp.float32)
    noise_edge = (math.sqrt(DETS) + math.sqrt(NT)) / math.sqrt(DETS * NT)
    strength = jnp.exp(jax.random.uniform(keys[3], (K,), jnp.float32, math.log(1.2), math.log(4.0))) * noise_edge
    common = jnp.dot(mixing * strength[None, :], mode_rows, precision=lax.Precision.HIGHEST)
    result = white_noise + common
    return jnp.clip(result, -12.0, 12.0)


def draw_pointing(key, part):
    keys = jax.random.split(jax.random.fold_in(key, 202), 2)
    det_group = jnp.arange(DETS, dtype=jnp.int32) // DET_DEV
    scan_step = jax.random.randint(keys[0], (DETS, NT), 0, 4, dtype=jnp.int32)
    offset = jax.random.randint(keys[1], (DETS, NT), 0, PB, dtype=jnp.int32)
    return ((det_group[:, None] + scan_step) % NBLK * PB + offset).astype(jnp.int32)


def set_ends(values, rng, low, top_value):
    longest = values.shape.index(max(values.shape))
    spots = []
    for shift in (0, 1):
        where = [jax.random.randint(jax.random.fold_in(rng, axis), (), 0, length) for axis, length in enumerate(values.shape)]
        where[longest] = (where[longest] + shift) % values.shape[longest]
        spots.append(tuple(where))
    return values.at[spots[0]].set(low).at[spots[1]].set(top_value)


def levels(stream_key, dims, cuts, low, largest):
    def one(position, blocks):
        steps = jax.random.uniform(jax.random.fold_in(jax.random.fold_in(stream_key, 6), position), (blocks,), jnp.float32, low / len(cuts), largest / len(cuts))
        return jnp.repeat(jnp.exp(steps), dims[position] // blocks).reshape((-1,) + (1,) * (len(dims) - position - 1))

    gain = one(*cuts[0])
    for cut in cuts[1:]:
        gain = gain * one(*cut)
    return gain


def bell_draw(own_key, extent, deviation, bound, held_as=jnp.bfloat16):
    values = jax.random.normal(own_key, extent, jnp.float32) * deviation
    return jnp.minimum(jnp.maximum(values, -bound), bound).astype(held_as)


def setup_inputs(seed: int = 0, part: int = 0) -> dict:
    seeds = jax.random.split(jax.random.key(seed), 7)
    part_splits = jax.random.split(jax.random.fold_in(seeds[6], part), 7)
    timestreams = draw_timestreams(jax.random.fold_in(jax.random.fold_in(seeds[6], part), 71), part)
    pointing = draw_pointing(jax.random.fold_in(jax.random.fold_in(seeds[6], part), 71), part)
    det_flags = set_ends((jax.random.randint(part_splits[2], (DETS,), 0, 8) < 7).astype(jnp.int32), jax.random.fold_in(part_splits[2], 1), 0, 1)
    det_weight = jnp.clip(jnp.exp(math.log(2.0) - 2.3025851 * jax.random.uniform(part_splits[3], (DETS,), jnp.float32) ** levels(part_splits[3], (DETS,), ((0, 32),), -0.2, 0.2)), 0.2, 2.0)
    block_slot = jax.random.permutation(seeds[4], NBLK).astype(jnp.int32)
    start_modes = bell_draw(seeds[5], (NT, K), 1.0, 6.0, jnp.float32)
    return {"timestreams": timestreams, "pointing": pointing, "det_flags": det_flags, "det_weight": det_weight, "block_slot": block_slot, "start_modes": start_modes}


def orthonormal(tall_block):
    orthogonal, upper = jnp.linalg.qr(tall_block)
    return orthogonal * jnp.sign(jnp.diagonal(upper))[None, :]

def reference(timestreams, pointing, det_flags, det_weight, block_slot, start_modes):
    highest = lax.Precision.HIGHEST
    flag_value = det_flags.astype(jnp.float32)
    masked = timestreams * flag_value[:, None]
    time_basis = start_modes
    for repeat in range(ITERS):
        mixing = jnp.dot(masked.astype(jnp.float32), time_basis.astype(jnp.float32), precision=highest, preferred_element_type=jnp.float32)
        summed = jnp.dot(masked.T.astype(jnp.float32), mixing.astype(jnp.float32), precision=highest, preferred_element_type=jnp.float32)
        time_basis = orthonormal(summed)
    amplitude = jnp.dot(masked.astype(jnp.float32), time_basis.astype(jnp.float32), precision=highest, preferred_element_type=jnp.float32)
    cleaned = masked - jnp.dot(amplitude.astype(jnp.float32), time_basis.T.astype(jnp.float32), precision=highest, preferred_element_type=jnp.float32)
    detector_gain = det_weight * flag_value
    sample_weight = detector_gain.astype(jnp.bfloat16)
    weighted = (detector_gain[:, None] * cleaned).astype(jnp.bfloat16)
    pixel_slot = (block_slot[pointing // PB] * PB + pointing % PB).astype(jnp.int32)
    pixel_total = NBLK * PB
    signal_sum = jax.ops.segment_sum(weighted.astype(jnp.float32).reshape(-1), pixel_slot.reshape(-1), num_segments=pixel_total)
    weights_all = jnp.broadcast_to(sample_weight.astype(jnp.float32)[:, None], pointing.shape)
    weight_sum = jax.ops.segment_sum(weights_all.reshape(-1), pixel_slot.reshape(-1), num_segments=pixel_total)
    expected_hits = DET_DEV * NT / PB
    modes = jnp.sqrt(jnp.float32(NT)) * time_basis
    signal_map = (signal_sum / jnp.sqrt(jnp.float32(expected_hits))).reshape(NBLK, PB)
    weight_map = (weight_sum / jnp.float32(expected_hits)).reshape(NBLK, PB)
    return (modes, signal_map, weight_map)
```

```python
import functools
import math

import jax
import jax.numpy as jnp
from jax import lax
from jax.experimental import pallas as pl
from jax.experimental.pallas import tpu as pltpu
from jax.sharding import PartitionSpec as P

ITERS = 2
PB = 128


HIGHEST = lax.Precision.HIGHEST
REACH = 4


def project(masked, time_basis):
    partial_value = jnp.dot(
        masked, time_basis, precision=HIGHEST, preferred_element_type=jnp.float32
    )
    return lax.psum(partial_value, "tm")


def cholesky_pass(tall_block):
    gram_part = lax.dot_general(
        tall_block,
        tall_block,
        (((0,), (0,)), ((), ())),
        precision=HIGHEST,
        preferred_element_type=jnp.float32,
    )
    gram_total = lax.psum(gram_part, "tm")
    cholesky_low = jnp.linalg.cholesky(gram_total)
    return lax.linalg.triangular_solve(
        cholesky_low, tall_block, left_side=False, lower=True, transpose_a=True
    )


def orthonormal_rows(tall_block):
    tall_block = cholesky_pass(tall_block)
    return tall_block


def shards(timestreams, pointing, det_flags, det_weight, block_slot, start_modes):
    det_rows, time_cols = timestreams.shape
    total_time = time_cols * lax.axis_size("tm")
    flag_value = det_flags.astype(jnp.float32)
    masked = timestreams * flag_value[:, None]
    time_basis = start_modes
    for repeat in range(ITERS):
        mixing = project(masked, time_basis)
        partial_value = lax.dot_general(
            masked,
            mixing,
            (((0,), (0,)), ((), ())),
            precision=HIGHEST,
            preferred_element_type=jnp.float32,
        )
        summed = lax.psum(partial_value, "det")
        time_basis = orthonormal_rows(summed)
    amplitude = project(masked, time_basis)
    cleaned = masked - lax.dot_general(
        amplitude,
        time_basis,
        (((1,), (1,)), ((), ())),
        precision=HIGHEST,
        preferred_element_type=jnp.float32,
    )
    detector_gain = det_weight * flag_value
    sample_weight = detector_gain.astype(jnp.bfloat16)
    weighted = (detector_gain[:, None] * cleaned).astype(jnp.bfloat16)
    block_total = block_slot.shape[0]
    det_index = lax.axis_index("det")
    reach_ids = jnp.arange(REACH, dtype=jnp.int32)
    reach_rank = (pointing // PB - det_index) % block_total
    within = pointing % PB
    rows_per = math.gcd(det_rows, max(1, 4096 // time_cols))
    step_count = det_rows // rows_per
    pixel_iota = jnp.arange(PB, dtype=jnp.int32)
    nothing = jnp.zeros((), jnp.bfloat16)

    def accumulate(position, running):
        first_row = position * rows_per
        ranks = lax.dynamic_slice_in_dim(reach_rank, first_row, rows_per, 0).reshape(-1)
        offsets = lax.dynamic_slice_in_dim(within, first_row, rows_per, 0).reshape(-1)
        values = lax.dynamic_slice_in_dim(weighted, first_row, rows_per, 0).reshape(-1)
        weights_here = jnp.broadcast_to(
            lax.dynamic_slice_in_dim(sample_weight, first_row, rows_per, 0)[:, None],
            (rows_per, time_cols),
        ).reshape(-1)
        target = (ranks[:, None] == reach_ids[None, :]).astype(jnp.bfloat16)
        within_hot = offsets[:, None] == pixel_iota[None, :]
        paired = jnp.concatenate(
            [
                jnp.where(within_hot, values[:, None], nothing),
                jnp.where(within_hot, weights_here[:, None], nothing),
            ],
            axis=1,
        )
        return running + lax.dot_general(
            target, paired, (((0,), (0,)), ((), ())), preferred_element_type=jnp.float32
        )

    local_bins = lax.fori_loop(0, step_count, accumulate, jnp.zeros((REACH, 2 * PB), jnp.float32))
    local_bins = lax.psum(local_bins, "tm")
    block_iota = jnp.arange(block_total, dtype=jnp.int32)
    reached_blocks = (det_index + reach_ids) % block_total
    slot_of_reach = jnp.sum(
        jnp.where(block_iota[None, :] == reached_blocks[:, None], block_slot[None, :], 0), axis=1
    )
    placement = (block_iota[:, None] == slot_of_reach[None, :]).astype(jnp.float32)
    full_map = jnp.dot(placement, local_bins, precision=HIGHEST, preferred_element_type=jnp.float32)
    summed_map = lax.psum_scatter(full_map, "det", scatter_dimension=0, tiled=True)
    expected_hits = det_rows * total_time / PB
    signal_map = summed_map[:, :PB] / jnp.float32(math.sqrt(expected_hits))
    weight_map = summed_map[:, PB:] / jnp.float32(expected_hits)
    modes = jnp.float32(math.sqrt(total_time)) * time_basis
    return (modes, signal_map, weight_map)


SUB = 8
LANE = 128
LOOK = 4
LOW = 16


def dot(left, right, dims=(1, 0)):
    return lax.dot_general(
        left,
        right,
        (((dims[0],), (dims[1],)), ((), ())),
        precision=HIGHEST,
        preferred_element_type=jnp.float32,
    )


def spread_row(tile, row):
    return jnp.broadcast_to(tile[row : row + 1, :], tile.shape)


def inverse_factor(tall_t):
    size = tall_t.shape[0]
    padded = jnp.concatenate([tall_t, jnp.zeros_like(tall_t)], axis=0)
    gram = dot(tall_t, padded, (1, 1))
    row_id = lax.broadcasted_iota(jnp.int32, (size, 2 * size), 0)
    lane_id = lax.broadcasted_iota(jnp.int32, (size, 2 * size), 1)
    whole = jnp.where(lane_id == row_id + size, 1.0, gram)
    count = size // SUB
    tiles = [whole[SUB * i : SUB * (i + 1), :] for i in range(count)]
    in_tile = lax.broadcasted_iota(jnp.int32, (SUB, 2 * size), 0)
    for start in range(0, size, LOOK):
        first = start // SUB
        base = start % SUB
        columns = [
            {
                i: jnp.broadcast_to(tiles[i][:, start + q : start + q + 1], (SUB, 2 * size))
                for i in range(first, count)
            }
            for q in range(LOOK)
        ]
        rows = [spread_row(tiles[first], base + q) for q in range(LOOK)]
        corner = {
            (i, j): spread_row(columns[j][first], base + i) for j in range(LOOK) for i in range(j, LOOK)
        }
        scaled = []
        for q in range(LOOK):
            inverse = 1.0 / corner[q, q]
            scaled.append(rows[q] * inverse)
            factor = {i: corner[i, q] * inverse for i in range(q + 1, LOOK)}
            for j in range(q + 1, LOOK):
                for i in range(j, LOOK):
                    corner[i, j] = corner[i, j] - corner[i, q] * factor[j]
                rows[j] = rows[j] - factor[j] * rows[q]
                for i in range(first, count):
                    columns[j][i] = columns[j][i] - columns[q][i] * factor[j]
        for i in range(first, count):
            tile = tiles[i]
            for q in range(LOOK):
                column = columns[q][i]
                if i == first:
                    column = jnp.where(in_tile > base + q, column, 0.0)
                tile = tile - column * scaled[q]
            tiles[i] = tile
    whole = jnp.concatenate(tiles, axis=0)
    pivots = jnp.sum(jnp.where(lane_id == row_id, whole, 0.0), axis=1, keepdims=True)
    return whole * (1.0 / jnp.sqrt(pivots))


def apply_factor(factor, tall_t):
    return dot(factor, jnp.concatenate([jnp.zeros_like(tall_t), tall_t], axis=0))


def kernel(
    peers, slot_ref, data_ref, point_ref, flag_ref, weight_ref, start_ref,
    modes_ref, signal_ref, hits_ref,
    masked_ref, values_ref, high_ref, low_ref, pieces_ref, reduced_ref, bins_ref,
    part1_ref, full1_ref, part2_ref, full2_ref, maps_ref, send_sem, recv_sem,
):
    me = lax.axis_index("det")
    det_rows, time_cols = data_ref.shape
    size = start_ref.shape[1]
    across = time_cols // LANE

    barrier = pltpu.get_barrier_semaphore()

    def greet(step, carry):
        pl.semaphore_signal(
            barrier, inc=1, device_id={"det": lax.rem(me + step, peers)},
            device_id_type=pl.DeviceIdType.MESH,
        )
        return carry

    lax.fori_loop(1, peers, greet, 0, unroll=True)

    def send_all(source, target, phase):
        def one(step, carry):
            peer = lax.rem(me + step, peers)
            pltpu.make_async_remote_copy(
                src_ref=source(peer),
                dst_ref=target.at[me],
                send_sem=send_sem.at[phase],
                recv_sem=recv_sem.at[phase],
                device_id={"det": peer},
                device_id_type=pl.DeviceIdType.MESH,
            ).start()
            return carry

        lax.fori_loop(1, peers, one, 0, unroll=True)

    def await_bytes(target, sem):
        span = target.at[pl.ds(0, peers - 1)]
        pltpu.make_async_copy(span, span, sem).wait()

    def split(value):
        for i in range(size // SUB):
            for c in range(across):
                pieces_ref[i * across + c] = value[SUB * i : SUB * (i + 1), LANE * c : LANE * (c + 1)]

    def join(ref):
        return jnp.concatenate(
            [
                jnp.concatenate([ref[i * across + c] for c in range(across)], axis=1)
                for i in range(size // SUB)
            ],
            axis=0,
        )

    square = (det_rows, det_rows)
    diagonal = lax.broadcasted_iota(jnp.int32, square, 0) == lax.broadcasted_iota(jnp.int32, square, 1)

    def as_column(row):
        return jnp.sum(jnp.where(diagonal, jnp.broadcast_to(row, square), 0.0), axis=1, keepdims=True)

    flags = flag_ref[...].astype(jnp.float32)
    flag_column = as_column(flags)
    gain_column = as_column(weight_ref[...] * flags)
    masked_ref[...] = data_ref[...] * flag_column
    mixing = dot(masked_ref[...], start_ref[...])
    split(dot(mixing.T, masked_ref[...]))
    pl.semaphore_wait(barrier, peers - 1)
    send_all(lambda peer: pieces_ref.at[peer], part1_ref, 0)

    total = peers * PB
    high_rows = high_ref.shape[1]
    high_iota = lax.broadcasted_iota(jnp.int32, (high_rows, time_cols), 0)
    low_iota = lax.broadcasted_iota(jnp.int32, (LOW, time_cols), 0)

    def encode(group, carry):
        first = pl.multiple_of(group * SUB, SUB)
        place = point_ref[pl.ds(first, SUB), :] - me * PB
        place = jnp.where(place < 0, place + total, place)
        high = lax.shift_right_logical(place, 4)
        low = place & (LOW - 1)
        for r in range(SUB):
            high_hot = jnp.broadcast_to(high[r : r + 1, :], high_iota.shape) == high_iota
            low_hot = jnp.broadcast_to(low[r : r + 1, :], low_iota.shape) == low_iota
            high_ref[first + r] = jnp.where(high_hot, 1.0, 0.0).astype(jnp.bfloat16)
            low_ref[first + r] = jnp.where(low_hot, 1.0, 0.0).astype(jnp.bfloat16)
        return carry

    lax.fori_loop(0, det_rows // SUB, encode, 0)

    def binned():
        def one(group, running):
            first = pl.multiple_of(group * SUB, SUB)
            values = values_ref[pl.ds(first, SUB), :]
            for r in range(SUB):
                value = jnp.broadcast_to(values[r : r + 1, :], low_iota.shape)
                hot = low_ref[first + r].astype(jnp.float32)
                running = running + lax.dot_general(
                    high_ref[first + r], (hot * value).astype(jnp.bfloat16),
                    (((1,), (1,)), ((), ())), preferred_element_type=jnp.float32,
                )
            return running

        compact = lax.fori_loop(
            0, det_rows // SUB, one, jnp.zeros((high_rows, LOW), jnp.float32)
        )
        pick = lax.broadcasted_iota(jnp.int32, (LOW, PB), 1) % LOW == lax.broadcasted_iota(
            jnp.int32, (LOW, PB), 0
        )
        wide = dot(compact, jnp.where(pick, 1.0, 0.0))
        wide_shape = (high_rows, PB)
        keep = lax.broadcasted_iota(jnp.int32, wide_shape, 1) // LOW == lax.broadcasted_iota(
            jnp.int32, wide_shape, 0
        ) % (PB // LOW)
        wide = jnp.where(keep, wide, 0.0)
        per = PB // LOW
        return [
            jnp.sum(wide[per * r : per * (r + 1), :], axis=0, keepdims=True) for r in range(REACH)
        ]

    def reduce(ref, phase):
        ref[me] = pieces_ref[me]
        await_bytes(ref, recv_sem.at[phase])
        value = ref[0]
        for i in range(1, peers):
            value = value + ref[i]
        return value

    reduced_ref[0] = reduce(part1_ref, 0)
    send_all(lambda peer: reduced_ref.at[0], full1_ref, 1)
    values_ref[...] = jnp.broadcast_to(gain_column, values_ref.shape)
    weight_rows = binned()
    full1_ref[me] = reduced_ref[0]
    await_bytes(pieces_ref, send_sem.at[0])
    await_bytes(full1_ref, recv_sem.at[1])
    first_sum = join(full1_ref)

    split(dot(dot(first_sum, masked_ref[...], (1, 1)), masked_ref[...]))
    send_all(lambda peer: pieces_ref.at[peer], part2_ref, 2)
    factor = inverse_factor(first_sum)
    reduced_ref[1] = reduce(part2_ref, 2)
    send_all(lambda peer: reduced_ref.at[1], full2_ref, 3)
    full2_ref[me] = reduced_ref[1]
    await_bytes(full2_ref, recv_sem.at[3])
    second_sum = apply_factor(factor, join(full2_ref))
    basis_t = apply_factor(inverse_factor(second_sum), second_sum)
    modes_ref[...] = basis_t * math.sqrt(time_cols)

    masked = masked_ref[...]
    amplitude = dot(masked, basis_t, (1, 1))
    values_ref[...] = gain_column * (masked - dot(amplitude, basis_t))
    bins_ref[...] = jnp.concatenate(binned() + weight_rows, axis=0)
    send_all(lambda peer: bins_ref, maps_ref, 4)
    maps_ref[me] = bins_ref[...]

    def find(position, running):
        return running + jnp.where(slot_ref[0, position] == me, position, 0)

    block = lax.fori_loop(0, peers, find, jnp.int32(0), unroll=True)
    await_bytes(maps_ref, recv_sem.at[4])
    signal = jnp.zeros((1, PB), jnp.float32)
    hits = jnp.zeros((1, PB), jnp.float32)
    for r in range(REACH):
        tile = maps_ref[lax.rem(block - r + peers, peers)]
        signal = signal + tile[r : r + 1, :]
        hits = hits + tile[REACH + r : REACH + r + 1, :]
    expected_hits = det_rows * time_cols / PB
    signal_ref[...] = signal * (1.0 / math.sqrt(expected_hits))
    hits_ref[...] = hits * (1.0 / expected_hits)
    await_bytes(full1_ref, send_sem.at[1])
    await_bytes(part2_ref, send_sem.at[2])
    await_bytes(full2_ref, send_sem.at[3])
    await_bytes(maps_ref, send_sem.at[4])


def fused_shards(timestreams, pointing, det_flags, det_weight, block_slot, start_modes):
    peers = lax.axis_size("det")
    det_rows, time_cols = timestreams.shape
    size = start_modes.shape[1]
    stack = pltpu.VMEM((peers, SUB, LANE), jnp.float32)
    vmem = pl.BlockSpec(memory_space=pltpu.VMEM)
    modes_t, signal_map, weight_map = pl.pallas_call(
        functools.partial(kernel, peers),
        out_shape=(
            jax.ShapeDtypeStruct((size, time_cols), jnp.float32),
            jax.ShapeDtypeStruct((1, PB), jnp.float32),
            jax.ShapeDtypeStruct((1, PB), jnp.float32),
        ),
        in_specs=[pl.BlockSpec(memory_space=pltpu.SMEM)] + [vmem] * 5,
        out_specs=(vmem, vmem, vmem),
        scratch_shapes=[
            pltpu.VMEM((det_rows, time_cols), jnp.float32),
            pltpu.VMEM((det_rows, time_cols), jnp.float32),
            pltpu.VMEM((det_rows, REACH * PB // LOW, time_cols), jnp.bfloat16),
            pltpu.VMEM((det_rows, LOW, time_cols), jnp.bfloat16),
            stack,
            pltpu.VMEM((2, SUB, LANE), jnp.float32),
            pltpu.VMEM((SUB, LANE), jnp.float32),
            stack,
            stack,
            stack,
            stack,
            stack,
            pltpu.SemaphoreType.DMA((5,)),
            pltpu.SemaphoreType.DMA((5,)),
        ],
        compiler_params=pltpu.CompilerParams(
            collective_id=0, has_side_effects=True, vmem_limit_bytes=32 * 1024 * 1024
        ),
    )(
        block_slot.reshape(1, -1),
        timestreams,
        pointing,
        det_flags.reshape(1, -1),
        det_weight.reshape(1, -1),
        start_modes,
    )
    return modes_t.T, signal_map, weight_map


def fits(mesh, timestreams, block_slot, start_modes):
    peers = mesh.shape["det"]
    size = start_modes.shape[1]
    return (
        mesh.shape["tm"] == 1
        and block_slot.shape[0] == peers
        and peers > REACH
        and timestreams.shape[1] * size == peers * SUB * LANE
        and 2 * size == LANE
        and timestreams.shape[0] // (peers * mesh.shape["obs"]) % SUB == 0
    )


def solution(mesh):
    def run(timestreams, pointing, det_flags, det_weight, block_slot, start_modes):
        body = fused_shards if fits(mesh, timestreams, block_slot, start_modes) else shards
        return jax.shard_map(
            body,
            mesh=mesh,
            in_specs=(
                P(("obs", "det"), "tm"),
                P(("obs", "det"), "tm"),
                P(("obs", "det")),
                P(("obs", "det")),
                P(),
                P("tm", None),
            ),
            out_specs=(P(("obs", "tm"), None), P(("obs", "det"), None), P(("obs", "det"), None)),
            check_vma=False,
        )(timestreams, pointing, det_flags, det_weight, block_slot, start_modes)

    return run
```

```python
import functools
import math

import jax
import jax.numpy as jnp
from jax import lax
from jax.experimental import pallas as pl
from jax.experimental.pallas import tpu as pltpu
from jax.sharding import PartitionSpec as P

ITERS = 2
PB = 128


HIGHEST = lax.Precision.HIGHEST
REACH = 4


def project(masked, time_basis):
    partial_value = jnp.dot(
        masked, time_basis, precision=HIGHEST, preferred_element_type=jnp.float32
    )
    return lax.psum(partial_value, "tm")


def cholesky_pass(tall_block):
    gram_part = lax.dot_general(
        tall_block,
        tall_block,
        (((0,), (0,)), ((), ())),
        precision=HIGHEST,
        preferred_element_type=jnp.float32,
    )
    gram_total = lax.psum(gram_part, "tm")
    cholesky_low = jnp.linalg.cholesky(gram_total)
    return lax.linalg.triangular_solve(
        cholesky_low, tall_block, left_side=False, lower=True, transpose_a=True
    )


def orthonormal_rows(tall_block):
    tall_block = cholesky_pass(tall_block)
    return tall_block


def shards(timestreams, pointing, det_flags, det_weight, block_slot, start_modes):
    det_rows, time_cols = timestreams.shape
    total_time = time_cols * lax.axis_size("tm")
    flag_value = det_flags.astype(jnp.float32)
    masked = timestreams * flag_value[:, None]
    time_basis = start_modes
    for repeat in range(ITERS):
        mixing = project(masked, time_basis)
        partial_value = lax.dot_general(
            masked,
            mixing,
            (((0,), (0,)), ((), ())),
            precision=HIGHEST,
            preferred_element_type=jnp.float32,
        )
        summed = lax.psum(partial_value, "det")
        time_basis = orthonormal_rows(summed)
    amplitude = project(masked, time_basis)
    cleaned = masked - lax.dot_general(
        amplitude,
        time_basis,
        (((1,), (1,)), ((), ())),
        precision=HIGHEST,
        preferred_element_type=jnp.float32,
    )
    detector_gain = det_weight * flag_value
    sample_weight = detector_gain.astype(jnp.bfloat16)
    weighted = (detector_gain[:, None] * cleaned).astype(jnp.bfloat16)
    block_total = block_slot.shape[0]
    det_index = lax.axis_index("det")
    reach_ids = jnp.arange(REACH, dtype=jnp.int32)
    reach_rank = (pointing // PB - det_index) % block_total
    within = pointing % PB
    rows_per = math.gcd(det_rows, max(1, 4096 // time_cols))
    step_count = det_rows // rows_per
    pixel_iota = jnp.arange(PB, dtype=jnp.int32)
    nothing = jnp.zeros((), jnp.bfloat16)

    def accumulate(position, running):
        first_row = position * rows_per
        ranks = lax.dynamic_slice_in_dim(reach_rank, first_row, rows_per, 0).reshape(-1)
        offsets = lax.dynamic_slice_in_dim(within, first_row, rows_per, 0).reshape(-1)
        values = lax.dynamic_slice_in_dim(weighted, first_row, rows_per, 0).reshape(-1)
        weights_here = jnp.broadcast_to(
            lax.dynamic_slice_in_dim(sample_weight, first_row, rows_per, 0)[:, None],
            (rows_per, time_cols),
        ).reshape(-1)
        target = (ranks[:, None] == reach_ids[None, :]).astype(jnp.bfloat16)
        within_hot = offsets[:, None] == pixel_iota[None, :]
        paired = jnp.concatenate(
            [
                jnp.where(within_hot, values[:, None], nothing),
                jnp.where(within_hot, weights_here[:, None], nothing),
            ],
            axis=1,
        )
        return running + lax.dot_general(
            target, paired, (((0,), (0,)), ((), ())), preferred_element_type=jnp.float32
        )

    local_bins = lax.fori_loop(0, step_count, accumulate, jnp.zeros((REACH, 2 * PB), jnp.float32))
    local_bins = lax.psum(local_bins, "tm")
    block_iota = jnp.arange(block_total, dtype=jnp.int32)
    reached_blocks = (det_index + reach_ids) % block_total
    slot_of_reach = jnp.sum(
        jnp.where(block_iota[None, :] == reached_blocks[:, None], block_slot[None, :], 0), axis=1
    )
    placement = (block_iota[:, None] == slot_of_reach[None, :]).astype(jnp.float32)
    full_map = jnp.dot(placement, local_bins, precision=HIGHEST, preferred_element_type=jnp.float32)
    summed_map = lax.psum_scatter(full_map, "det", scatter_dimension=0, tiled=True)
    expected_hits = det_rows * total_time / PB
    signal_map = summed_map[:, :PB] / jnp.float32(math.sqrt(expected_hits))
    weight_map = summed_map[:, PB:] / jnp.float32(expected_hits)
    modes = jnp.float32(math.sqrt(total_time)) * time_basis
    return (modes, signal_map, weight_map)


SUB = 8
LANE = 128
LOOK = 4
LOW = 16


def dot(left, right, dims=(1, 0)):
    return lax.dot_general(
        left,
        right,
        (((dims[0],), (dims[1],)), ((), ())),
        precision=HIGHEST,
        preferred_element_type=jnp.float32,
    )


def partner(me, step, peers):
    if peers & (peers - 1) == 0:
        return me ^ (peers - step)
    return lax.rem(me + (peers - step), peers)


def spread_row(tile, row):
    return jnp.broadcast_to(tile[row : row + 1, :], tile.shape)


def inverse_factor(tall_t):
    size = tall_t.shape[0]
    padded = jnp.concatenate([tall_t, jnp.zeros_like(tall_t)], axis=0)
    gram = dot(tall_t, padded, (1, 1))
    row_id = lax.broadcasted_iota(jnp.int32, (size, 2 * size), 0)
    lane_id = lax.broadcasted_iota(jnp.int32, (size, 2 * size), 1)
    whole = jnp.where(lane_id == row_id + size, 1.0, gram)
    count = size // SUB
    tiles = [whole[SUB * i : SUB * (i + 1), :] for i in range(count)]
    in_tile = lax.broadcasted_iota(jnp.int32, (SUB, 2 * size), 0)
    for start in range(0, size, LOOK):
        first = start // SUB
        base = start % SUB
        columns = [
            {
                i: jnp.broadcast_to(tiles[i][:, start + q : start + q + 1], (SUB, 2 * size))
                for i in range(first, count)
            }
            for q in range(LOOK)
        ]
        rows = [spread_row(tiles[first], base + q) for q in range(LOOK)]
        corner = {
            (i, j): spread_row(columns[j][first], base + i) for j in range(LOOK) for i in range(j, LOOK)
        }
        scaled = []
        for q in range(LOOK):
            inverse = 1.0 / corner[q, q]
            scaled.append(rows[q] * inverse)
            factor = {i: corner[i, q] * inverse for i in range(q + 1, LOOK)}
            for j in range(q + 1, LOOK):
                for i in range(j, LOOK):
                    corner[i, j] = corner[i, j] - corner[i, q] * factor[j]
                rows[j] = rows[j] - factor[j] * rows[q]
                for i in range(first, count):
                    columns[j][i] = columns[j][i] - columns[q][i] * factor[j]
        for i in range(first, count):
            tile = tiles[i]
            for q in range(LOOK):
                column = columns[q][i]
                if i == first:
                    column = jnp.where(in_tile > base + q, column, 0.0)
                tile = tile - column * scaled[q]
            tiles[i] = tile
    whole = jnp.concatenate(tiles, axis=0)
    pivots = jnp.sum(jnp.where(lane_id == row_id, whole, 0.0), axis=1, keepdims=True)
    return whole * (1.0 / jnp.sqrt(pivots))


def apply_factor(factor, tall_t):
    return dot(factor, jnp.concatenate([jnp.zeros_like(tall_t), tall_t], axis=0))


def kernel(
    peers, slot_ref, data_ref, point_ref, flag_ref, weight_ref, start_ref,
    modes_ref, signal_ref, hits_ref,
    masked_ref, values_ref, high_ref, low_ref, pieces_ref, reduced_ref, weights_ref, bins_ref,
    part1_ref, full1_ref, part2_ref, full2_ref, hit_maps_ref, maps_ref, send_sem, recv_sem,
):
    me = lax.axis_index("det")
    det_rows, time_cols = data_ref.shape
    size = start_ref.shape[0]
    across = time_cols // LANE

    barrier = pltpu.get_barrier_semaphore()

    def greet(step, carry):
        pl.semaphore_signal(
            barrier, inc=1, device_id={"det": partner(me, step, peers)},
            device_id_type=pl.DeviceIdType.MESH,
        )
        return carry

    lax.fori_loop(1, peers, greet, 0, unroll=True)

    def send_all(source, target, phase):
        def one(step, carry):
            peer = partner(me, step, peers)
            pltpu.make_async_remote_copy(
                src_ref=source(peer),
                dst_ref=target.at[me],
                send_sem=send_sem.at[phase],
                recv_sem=recv_sem.at[phase],
                device_id={"det": peer},
                device_id_type=pl.DeviceIdType.MESH,
            ).start()
            return carry

        lax.fori_loop(1, peers, one, 0, unroll=True)

    def await_bytes(target, sem):
        span = target.at[pl.ds(0, peers - 1)]
        pltpu.make_async_copy(span, span, sem).wait()

    def split(value):
        for i in range(size // SUB):
            for c in range(across):
                pieces_ref[i * across + c] = value[SUB * i : SUB * (i + 1), LANE * c : LANE * (c + 1)]

    def join(ref):
        return jnp.concatenate(
            [
                jnp.concatenate([ref[i * across + c] for c in range(across)], axis=1)
                for i in range(size // SUB)
            ],
            axis=0,
        )

    square = (det_rows, det_rows)
    diagonal = lax.broadcasted_iota(jnp.int32, square, 0) == lax.broadcasted_iota(jnp.int32, square, 1)

    def as_column(row):
        return jnp.sum(jnp.where(diagonal, jnp.broadcast_to(row, square), 0.0), axis=1, keepdims=True)

    flags = flag_ref[...].astype(jnp.float32)
    flag_column = as_column(flags)
    gain_column = as_column(weight_ref[...] * flags)
    masked_ref[...] = data_ref[...] * flag_column
    split(dot(dot(start_ref[...], masked_ref[...], (1, 1)), masked_ref[...]))
    pl.semaphore_wait(barrier, peers - 1)
    send_all(lambda peer: pieces_ref.at[peer], part1_ref, 0)

    total = peers * PB
    high_rows = high_ref.shape[1]
    high_iota = lax.broadcasted_iota(jnp.int32, (high_rows, time_cols), 0)
    low_iota = lax.broadcasted_iota(jnp.int32, (LOW, time_cols), 0)

    def encode(group, carry):
        first = pl.multiple_of(group * SUB, SUB)
        place = point_ref[pl.ds(first, SUB), :] - me * PB
        place = jnp.where(place < 0, place + total, place)
        high = lax.shift_right_logical(place, 4)
        low = place & (LOW - 1)
        for r in range(SUB):
            high_hot = jnp.broadcast_to(high[r : r + 1, :], high_iota.shape) == high_iota
            low_hot = jnp.broadcast_to(low[r : r + 1, :], low_iota.shape) == low_iota
            high_ref[first + r] = jnp.where(high_hot, 1.0, 0.0).astype(jnp.bfloat16)
            low_ref[first + r] = jnp.where(low_hot, 1.0, 0.0).astype(jnp.bfloat16)
        return carry

    lax.fori_loop(0, det_rows // SUB, encode, 0)

    def binned():
        def one(group, running):
            first = pl.multiple_of(group * SUB, SUB)
            values = values_ref[pl.ds(first, SUB), :]
            for r in range(SUB):
                value = jnp.broadcast_to(values[r : r + 1, :], low_iota.shape)
                hot = low_ref[first + r].astype(jnp.float32)
                running = running + lax.dot_general(
                    high_ref[first + r], (hot * value).astype(jnp.bfloat16),
                    (((1,), (1,)), ((), ())), preferred_element_type=jnp.float32,
                )
            return running

        compact = lax.fori_loop(
            0, det_rows // SUB, one, jnp.zeros((high_rows, LOW), jnp.float32)
        )
        pick = lax.broadcasted_iota(jnp.int32, (LOW, PB), 1) % LOW == lax.broadcasted_iota(
            jnp.int32, (LOW, PB), 0
        )
        wide = dot(compact, jnp.where(pick, 1.0, 0.0))
        wide_shape = (high_rows, PB)
        keep = lax.broadcasted_iota(jnp.int32, wide_shape, 1) // LOW == lax.broadcasted_iota(
            jnp.int32, wide_shape, 0
        ) % (PB // LOW)
        wide = jnp.where(keep, wide, 0.0)
        per = PB // LOW
        return [
            jnp.sum(wide[per * r : per * (r + 1), :], axis=0, keepdims=True) for r in range(REACH)
        ]

    def reduce(ref, phase):
        ref[me] = pieces_ref[me]
        await_bytes(ref, recv_sem.at[phase])
        values = [ref[i] for i in range(peers)]
        while len(values) > 1:
            pairs = [a + b for a, b in zip(values[::2], values[1::2])]
            values = pairs + values[len(pairs) * 2 :]
        return values[0]

    reduced_ref[0] = reduce(part1_ref, 0)
    send_all(lambda peer: reduced_ref.at[0], full1_ref, 1)
    values_ref[...] = jnp.broadcast_to(gain_column, values_ref.shape)
    weights_ref[...] = jnp.concatenate(binned(), axis=0)
    send_all(lambda peer: weights_ref, hit_maps_ref, 5)
    hit_maps_ref[me] = weights_ref[...]
    full1_ref[me] = reduced_ref[0]
    await_bytes(pieces_ref, send_sem.at[0])
    await_bytes(full1_ref, recv_sem.at[1])
    first_sum = join(full1_ref)

    split(dot(dot(first_sum, masked_ref[...], (1, 1)), masked_ref[...]))
    send_all(lambda peer: pieces_ref.at[peer], part2_ref, 2)
    factor = inverse_factor(first_sum)
    reduced_ref[1] = reduce(part2_ref, 2)
    send_all(lambda peer: reduced_ref.at[1], full2_ref, 3)
    full2_ref[me] = reduced_ref[1]
    await_bytes(full2_ref, recv_sem.at[3])
    second_sum = apply_factor(factor, join(full2_ref))
    basis_t = apply_factor(inverse_factor(second_sum), second_sum)
    modes_ref[...] = basis_t * math.sqrt(time_cols)

    masked = masked_ref[...]
    amplitude = dot(masked, basis_t, (1, 1))
    values_ref[...] = gain_column * (masked - dot(amplitude, basis_t))
    bins_ref[...] = jnp.concatenate(binned(), axis=0)
    send_all(lambda peer: bins_ref, maps_ref, 4)
    maps_ref[me] = bins_ref[...]

    def find(position, running):
        return running + jnp.where(slot_ref[0, position] == me, position, 0)

    block = lax.fori_loop(0, peers, find, jnp.int32(0), unroll=True)
    await_bytes(hit_maps_ref, recv_sem.at[5])
    await_bytes(maps_ref, recv_sem.at[4])
    signal = jnp.zeros((1, PB), jnp.float32)
    hits = jnp.zeros((1, PB), jnp.float32)
    for r in range(REACH):
        source = lax.rem(block - r + peers, peers)
        signal = signal + maps_ref[source][r : r + 1, :]
        hits = hits + hit_maps_ref[source][r : r + 1, :]
    expected_hits = det_rows * time_cols / PB
    signal_ref[...] = signal * (1.0 / math.sqrt(expected_hits))
    hits_ref[...] = hits * (1.0 / expected_hits)
    await_bytes(full1_ref, send_sem.at[1])
    await_bytes(part2_ref, send_sem.at[2])
    await_bytes(full2_ref, send_sem.at[3])
    await_bytes(maps_ref, send_sem.at[4])
    await_bytes(hit_maps_ref, send_sem.at[5])


def fused_shards(timestreams, pointing, det_flags, det_weight, block_slot, start_modes):
    peers = lax.axis_size("det")
    det_rows, time_cols = timestreams.shape
    size = start_modes.shape[1]
    stack = pltpu.VMEM((peers, SUB, LANE), jnp.float32)
    maps = pltpu.VMEM((peers, REACH, LANE), jnp.float32)
    vmem = pl.BlockSpec(memory_space=pltpu.VMEM)
    modes_t, signal_map, weight_map = pl.pallas_call(
        functools.partial(kernel, peers),
        out_shape=(
            jax.ShapeDtypeStruct((size, time_cols), jnp.float32),
            jax.ShapeDtypeStruct((1, PB), jnp.float32),
            jax.ShapeDtypeStruct((1, PB), jnp.float32),
        ),
        in_specs=[pl.BlockSpec(memory_space=pltpu.SMEM)] + [vmem] * 5,
        out_specs=(vmem, vmem, vmem),
        scratch_shapes=[
            pltpu.VMEM((det_rows, time_cols), jnp.float32),
            pltpu.VMEM((det_rows, time_cols), jnp.float32),
            pltpu.VMEM((det_rows, REACH * PB // LOW, time_cols), jnp.bfloat16),
            pltpu.VMEM((det_rows, LOW, time_cols), jnp.bfloat16),
            stack,
            pltpu.VMEM((2, SUB, LANE), jnp.float32),
            pltpu.VMEM((REACH, LANE), jnp.float32),
            pltpu.VMEM((REACH, LANE), jnp.float32),
            stack,
            stack,
            stack,
            stack,
            maps,
            maps,
            pltpu.SemaphoreType.DMA((6,)),
            pltpu.SemaphoreType.DMA((6,)),
        ],
        compiler_params=pltpu.CompilerParams(
            collective_id=0, has_side_effects=True, vmem_limit_bytes=32 * 1024 * 1024
        ),
    )(
        block_slot.reshape(1, -1),
        timestreams,
        pointing,
        det_flags.reshape(1, -1),
        det_weight.reshape(1, -1),
        start_modes.T,
    )
    return modes_t.T, signal_map, weight_map


def fits(mesh, timestreams, block_slot, start_modes):
    peers = mesh.shape["det"]
    size = start_modes.shape[1]
    return (
        mesh.shape["tm"] == 1
        and block_slot.shape[0] == peers
        and peers > REACH
        and timestreams.shape[1] * size == peers * SUB * LANE
        and 2 * size == LANE
        and timestreams.shape[0] // (peers * mesh.shape["obs"]) % SUB == 0
    )


def solution(mesh):
    def run(timestreams, pointing, det_flags, det_weight, block_slot, start_modes):
        body = fused_shards if fits(mesh, timestreams, block_slot, start_modes) else shards
        return jax.shard_map(
            body,
            mesh=mesh,
            in_specs=(
                P(("obs", "det"), "tm"),
                P(("obs", "det"), "tm"),
                P(("obs", "det")),
                P(("obs", "det")),
                P(),
                P("tm", None),
            ),
            out_specs=(P(("obs", "tm"), None), P(("obs", "det"), None), P(("obs", "det"), None)),
            check_vma=False,
        )(timestreams, pointing, det_flags, det_weight, block_slot, start_modes)

    return run
```

```python
import functools
import math

import jax
import jax.numpy as jnp
from jax import lax
from jax.experimental import pallas as pl
from jax.experimental.pallas import tpu as pltpu
from jax.sharding import PartitionSpec as P

ITERS = 2
PB = 128


HIGHEST = lax.Precision.HIGHEST
REACH = 4


def project(masked, time_basis):
    partial_value = jnp.dot(
        masked, time_basis, precision=HIGHEST, preferred_element_type=jnp.float32
    )
    return lax.psum(partial_value, "tm")


def cholesky_pass(tall_block):
    gram_part = lax.dot_general(
        tall_block,
        tall_block,
        (((0,), (0,)), ((), ())),
        precision=HIGHEST,
        preferred_element_type=jnp.float32,
    )
    gram_total = lax.psum(gram_part, "tm")
    cholesky_low = jnp.linalg.cholesky(gram_total)
    return lax.linalg.triangular_solve(
        cholesky_low, tall_block, left_side=False, lower=True, transpose_a=True
    )


def orthonormal_rows(tall_block):
    tall_block = cholesky_pass(tall_block)
    return tall_block


def shards(timestreams, pointing, det_flags, det_weight, block_slot, start_modes):
    det_rows, time_cols = timestreams.shape
    total_time = time_cols * lax.axis_size("tm")
    flag_value = det_flags.astype(jnp.float32)
    masked = timestreams * flag_value[:, None]
    time_basis = start_modes
    for repeat in range(ITERS):
        mixing = project(masked, time_basis)
        partial_value = lax.dot_general(
            masked,
            mixing,
            (((0,), (0,)), ((), ())),
            precision=HIGHEST,
            preferred_element_type=jnp.float32,
        )
        summed = lax.psum(partial_value, "det")
        time_basis = orthonormal_rows(summed)
    amplitude = project(masked, time_basis)
    cleaned = masked - lax.dot_general(
        amplitude,
        time_basis,
        (((1,), (1,)), ((), ())),
        precision=HIGHEST,
        preferred_element_type=jnp.float32,
    )
    detector_gain = det_weight * flag_value
    sample_weight = detector_gain.astype(jnp.bfloat16)
    weighted = (detector_gain[:, None] * cleaned).astype(jnp.bfloat16)
    block_total = block_slot.shape[0]
    det_index = lax.axis_index("det")
    reach_ids = jnp.arange(REACH, dtype=jnp.int32)
    reach_rank = (pointing // PB - det_index) % block_total
    within = pointing % PB
    rows_per = math.gcd(det_rows, max(1, 4096 // time_cols))
    step_count = det_rows // rows_per
    pixel_iota = jnp.arange(PB, dtype=jnp.int32)
    nothing = jnp.zeros((), jnp.bfloat16)

    def accumulate(position, running):
        first_row = position * rows_per
        ranks = lax.dynamic_slice_in_dim(reach_rank, first_row, rows_per, 0).reshape(-1)
        offsets = lax.dynamic_slice_in_dim(within, first_row, rows_per, 0).reshape(-1)
        values = lax.dynamic_slice_in_dim(weighted, first_row, rows_per, 0).reshape(-1)
        weights_here = jnp.broadcast_to(
            lax.dynamic_slice_in_dim(sample_weight, first_row, rows_per, 0)[:, None],
            (rows_per, time_cols),
        ).reshape(-1)
        target = (ranks[:, None] == reach_ids[None, :]).astype(jnp.bfloat16)
        within_hot = offsets[:, None] == pixel_iota[None, :]
        paired = jnp.concatenate(
            [
                jnp.where(within_hot, values[:, None], nothing),
                jnp.where(within_hot, weights_here[:, None], nothing),
            ],
            axis=1,
        )
        return running + lax.dot_general(
            target, paired, (((0,), (0,)), ((), ())), preferred_element_type=jnp.float32
        )

    local_bins = lax.fori_loop(0, step_count, accumulate, jnp.zeros((REACH, 2 * PB), jnp.float32))
    local_bins = lax.psum(local_bins, "tm")
    block_iota = jnp.arange(block_total, dtype=jnp.int32)
    reached_blocks = (det_index + reach_ids) % block_total
    slot_of_reach = jnp.sum(
        jnp.where(block_iota[None, :] == reached_blocks[:, None], block_slot[None, :], 0), axis=1
    )
    placement = (block_iota[:, None] == slot_of_reach[None, :]).astype(jnp.float32)
    full_map = jnp.dot(placement, local_bins, precision=HIGHEST, preferred_element_type=jnp.float32)
    summed_map = lax.psum_scatter(full_map, "det", scatter_dimension=0, tiled=True)
    expected_hits = det_rows * total_time / PB
    signal_map = summed_map[:, :PB] / jnp.float32(math.sqrt(expected_hits))
    weight_map = summed_map[:, PB:] / jnp.float32(expected_hits)
    modes = jnp.float32(math.sqrt(total_time)) * time_basis
    return (modes, signal_map, weight_map)


SUB = 8
LANE = 128
LOOK = 4
LOW = 16


def dot(left, right, dims=(1, 0)):
    return lax.dot_general(
        left,
        right,
        (((dims[0],), (dims[1],)), ((), ())),
        precision=HIGHEST,
        preferred_element_type=jnp.float32,
    )


def partner(me, step, peers):
    if peers & (peers - 1) == 0:
        return me ^ (peers - step)
    return lax.rem(me + (peers - step), peers)


def spread_row(tile, row):
    return jnp.broadcast_to(tile[row : row + 1, :], tile.shape)


def inverse_factor(tall_t):
    size = tall_t.shape[0]
    padded = jnp.concatenate([tall_t, jnp.zeros_like(tall_t)], axis=0)
    gram = dot(tall_t, padded, (1, 1))
    row_id = lax.broadcasted_iota(jnp.int32, (size, 2 * size), 0)
    lane_id = lax.broadcasted_iota(jnp.int32, (size, 2 * size), 1)
    whole = jnp.where(lane_id == row_id + size, 1.0, gram)
    count = size // SUB
    tiles = [whole[SUB * i : SUB * (i + 1), :] for i in range(count)]
    in_tile = lax.broadcasted_iota(jnp.int32, (SUB, 2 * size), 0)
    for start in range(0, size, LOOK):
        first = start // SUB
        base = start % SUB
        columns = [
            {
                i: jnp.broadcast_to(tiles[i][:, start + q : start + q + 1], (SUB, 2 * size))
                for i in range(first, count)
            }
            for q in range(LOOK)
        ]
        rows = [spread_row(tiles[first], base + q) for q in range(LOOK)]
        corner = {
            (i, j): spread_row(columns[j][first], base + i) for j in range(LOOK) for i in range(j, LOOK)
        }
        scaled = []
        for q in range(LOOK):
            inverse = 1.0 / corner[q, q]
            scaled.append(rows[q] * inverse)
            factor = {i: corner[i, q] * inverse for i in range(q + 1, LOOK)}
            for j in range(q + 1, LOOK):
                for i in range(j, LOOK):
                    corner[i, j] = corner[i, j] - corner[i, q] * factor[j]
                rows[j] = rows[j] - factor[j] * rows[q]
                for i in range(first, count):
                    columns[j][i] = columns[j][i] - columns[q][i] * factor[j]
        for i in range(first, count):
            tile = tiles[i]
            for q in range(LOOK):
                column = columns[q][i]
                if i == first:
                    column = jnp.where(in_tile > base + q, column, 0.0)
                tile = tile - column * scaled[q]
            tiles[i] = tile
    whole = jnp.concatenate(tiles, axis=0)
    pivots = jnp.sum(jnp.where(lane_id == row_id, whole, 0.0), axis=1, keepdims=True)
    return whole * (1.0 / jnp.sqrt(pivots))


def apply_factor(factor, tall_t):
    return dot(factor, jnp.concatenate([jnp.zeros_like(tall_t), tall_t], axis=0))


def kernel(
    peers, slot_hbm, data_hbm, point_hbm, flag_hbm, weight_hbm, start_hbm,
    modes_ref, signal_ref, hits_ref,
    slot_ref, data_ref, point_ref, flag_ref, weight_ref, start_ref, load_sem,
    masked_ref, values_ref, high_ref, low_ref, pieces_ref, reduced_ref, weights_ref, bins_ref,
    part1_ref, full1_ref, part2_ref, full2_ref, hit_maps_ref, maps_ref, send_sem, recv_sem,
):
    me = lax.axis_index("det")
    det_rows, time_cols = data_ref.shape
    size = start_ref.shape[0]
    across = time_cols // LANE

    barrier = pltpu.get_barrier_semaphore()

    def greet(step, carry):
        pl.semaphore_signal(
            barrier, inc=1, device_id={"det": partner(me, step, peers)},
            device_id_type=pl.DeviceIdType.MESH,
        )
        return carry

    loads = [
        pltpu.make_async_copy(source, target, load_sem.at[i])
        for i, (source, target) in enumerate(
            (
                (data_hbm, data_ref),
                (start_hbm, start_ref),
                (flag_hbm, flag_ref),
                (weight_hbm, weight_ref),
                (point_hbm, point_ref),
                (slot_hbm, slot_ref),
            )
        )
    ]
    for load in loads:
        load.start()
    lax.fori_loop(1, peers, greet, 0, unroll=True)

    def send_all(source, target, phase):
        def one(step, carry):
            peer = partner(me, step, peers)
            pltpu.make_async_remote_copy(
                src_ref=source(peer),
                dst_ref=target.at[me],
                send_sem=send_sem.at[phase],
                recv_sem=recv_sem.at[phase],
                device_id={"det": peer},
                device_id_type=pl.DeviceIdType.MESH,
            ).start()
            return carry

        lax.fori_loop(1, peers, one, 0, unroll=True)

    def await_bytes(target, sem):
        span = target.at[pl.ds(0, peers - 1)]
        pltpu.make_async_copy(span, span, sem).wait()

    def split(value):
        for i in range(size // SUB):
            for c in range(across):
                pieces_ref[i * across + c] = value[SUB * i : SUB * (i + 1), LANE * c : LANE * (c + 1)]

    def join(ref):
        return jnp.concatenate(
            [
                jnp.concatenate([ref[i * across + c] for c in range(across)], axis=1)
                for i in range(size // SUB)
            ],
            axis=0,
        )

    square = (det_rows, det_rows)
    diagonal = lax.broadcasted_iota(jnp.int32, square, 0) == lax.broadcasted_iota(jnp.int32, square, 1)

    def as_column(row):
        return jnp.sum(jnp.where(diagonal, jnp.broadcast_to(row, square), 0.0), axis=1, keepdims=True)

    for load in loads[:4]:
        load.wait()
    flags = flag_ref[...].astype(jnp.float32)
    flag_column = as_column(flags)
    gain_column = as_column(weight_ref[...] * flags)
    masked_ref[...] = data_ref[...] * flag_column
    split(dot(dot(start_ref[...], masked_ref[...], (1, 1)), masked_ref[...]))
    pl.semaphore_wait(barrier, peers - 1)
    send_all(lambda peer: pieces_ref.at[peer], part1_ref, 0)

    total = peers * PB
    for load in loads[4:]:
        load.wait()
    high_rows = high_ref.shape[1]
    high_iota = lax.broadcasted_iota(jnp.int32, (high_rows, time_cols), 0)
    low_iota = lax.broadcasted_iota(jnp.int32, (LOW, time_cols), 0)

    def encode(group, carry):
        first = pl.multiple_of(group * SUB, SUB)
        place = point_ref[pl.ds(first, SUB), :] - me * PB
        place = jnp.where(place < 0, place + total, place)
        high = lax.shift_right_logical(place, 4)
        low = place & (LOW - 1)
        for r in range(SUB):
            high_hot = jnp.broadcast_to(high[r : r + 1, :], high_iota.shape) == high_iota
            low_hot = jnp.broadcast_to(low[r : r + 1, :], low_iota.shape) == low_iota
            high_ref[first + r] = jnp.where(high_hot, 1.0, 0.0).astype(jnp.bfloat16)
            low_ref[first + r] = jnp.where(low_hot, 1.0, 0.0).astype(jnp.bfloat16)
        return carry

    lax.fori_loop(0, det_rows // SUB, encode, 0)

    def binned():
        def one(group, running):
            first = pl.multiple_of(group * SUB, SUB)
            values = values_ref[pl.ds(first, SUB), :]
            for r in range(SUB):
                value = jnp.broadcast_to(values[r : r + 1, :], low_iota.shape)
                hot = low_ref[first + r].astype(jnp.float32)
                running = running + lax.dot_general(
                    high_ref[first + r], (hot * value).astype(jnp.bfloat16),
                    (((1,), (1,)), ((), ())), preferred_element_type=jnp.float32,
                )
            return running

        compact = lax.fori_loop(
            0, det_rows // SUB, one, jnp.zeros((high_rows, LOW), jnp.float32)
        )
        pick = lax.broadcasted_iota(jnp.int32, (LOW, PB), 1) % LOW == lax.broadcasted_iota(
            jnp.int32, (LOW, PB), 0
        )
        wide = dot(compact, jnp.where(pick, 1.0, 0.0))
        wide_shape = (high_rows, PB)
        keep = lax.broadcasted_iota(jnp.int32, wide_shape, 1) // LOW == lax.broadcasted_iota(
            jnp.int32, wide_shape, 0
        ) % (PB // LOW)
        wide = jnp.where(keep, wide, 0.0)
        per = PB // LOW
        return [
            jnp.sum(wide[per * r : per * (r + 1), :], axis=0, keepdims=True) for r in range(REACH)
        ]

    def reduce(ref, phase):
        ref[me] = pieces_ref[me]
        await_bytes(ref, recv_sem.at[phase])
        values = [ref[i] for i in range(peers)]
        while len(values) > 1:
            pairs = [a + b for a, b in zip(values[::2], values[1::2])]
            values = pairs + values[len(pairs) * 2 :]
        return values[0]

    reduced_ref[0] = reduce(part1_ref, 0)
    send_all(lambda peer: reduced_ref.at[0], full1_ref, 1)
    values_ref[...] = jnp.broadcast_to(gain_column, values_ref.shape)
    weights_ref[...] = jnp.concatenate(binned(), axis=0)
    send_all(lambda peer: weights_ref, hit_maps_ref, 5)
    hit_maps_ref[me] = weights_ref[...]
    full1_ref[me] = reduced_ref[0]
    await_bytes(pieces_ref, send_sem.at[0])
    await_bytes(full1_ref, recv_sem.at[1])
    first_sum = join(full1_ref)

    split(dot(dot(first_sum, masked_ref[...], (1, 1)), masked_ref[...]))
    send_all(lambda peer: pieces_ref.at[peer], part2_ref, 2)
    factor = inverse_factor(first_sum)
    reduced_ref[1] = reduce(part2_ref, 2)
    send_all(lambda peer: reduced_ref.at[1], full2_ref, 3)
    full2_ref[me] = reduced_ref[1]
    await_bytes(full2_ref, recv_sem.at[3])
    second_sum = apply_factor(factor, join(full2_ref))
    basis_t = apply_factor(inverse_factor(second_sum), second_sum)
    modes_ref[...] = basis_t * math.sqrt(time_cols)

    masked = masked_ref[...]
    amplitude = dot(masked, basis_t, (1, 1))
    values_ref[...] = gain_column * (masked - dot(amplitude, basis_t))
    bins_ref[...] = jnp.concatenate(binned(), axis=0)
    send_all(lambda peer: bins_ref, maps_ref, 4)
    maps_ref[me] = bins_ref[...]

    def find(position, running):
        return running + jnp.where(slot_ref[0, position] == me, position, 0)

    block = lax.fori_loop(0, peers, find, jnp.int32(0), unroll=True)
    await_bytes(hit_maps_ref, recv_sem.at[5])
    await_bytes(maps_ref, recv_sem.at[4])
    signal = jnp.zeros((1, PB), jnp.float32)
    hits = jnp.zeros((1, PB), jnp.float32)
    for r in range(REACH):
        source = lax.rem(block - r + peers, peers)
        signal = signal + maps_ref[source][r : r + 1, :]
        hits = hits + hit_maps_ref[source][r : r + 1, :]
    expected_hits = det_rows * time_cols / PB
    signal_ref[...] = signal * (1.0 / math.sqrt(expected_hits))
    hits_ref[...] = hits * (1.0 / expected_hits)
    await_bytes(full1_ref, send_sem.at[1])
    await_bytes(part2_ref, send_sem.at[2])
    await_bytes(full2_ref, send_sem.at[3])
    await_bytes(maps_ref, send_sem.at[4])
    await_bytes(hit_maps_ref, send_sem.at[5])


def fused_shards(timestreams, pointing, det_flags, det_weight, block_slot, start_modes):
    peers = lax.axis_size("det")
    det_rows, time_cols = timestreams.shape
    size = start_modes.shape[1]
    stack = pltpu.VMEM((peers, SUB, LANE), jnp.float32)
    maps = pltpu.VMEM((peers, REACH, LANE), jnp.float32)
    vmem = pl.BlockSpec(memory_space=pltpu.VMEM)
    modes_t, signal_map, weight_map = pl.pallas_call(
        functools.partial(kernel, peers),
        out_shape=(
            jax.ShapeDtypeStruct((size, time_cols), jnp.float32),
            jax.ShapeDtypeStruct((1, PB), jnp.float32),
            jax.ShapeDtypeStruct((1, PB), jnp.float32),
        ),
        in_specs=[pl.BlockSpec(memory_space=pltpu.HBM)] * 6,
        out_specs=(vmem, vmem, vmem),
        scratch_shapes=[
            pltpu.SMEM((1, block_slot.shape[0]), jnp.int32),
            pltpu.VMEM((det_rows, time_cols), jnp.float32),
            pltpu.VMEM((det_rows, time_cols), jnp.int32),
            pltpu.VMEM((1, det_rows), jnp.int32),
            pltpu.VMEM((1, det_rows), jnp.float32),
            pltpu.VMEM((size, time_cols), jnp.float32),
            pltpu.SemaphoreType.DMA((6,)),
            pltpu.VMEM((det_rows, time_cols), jnp.float32),
            pltpu.VMEM((det_rows, time_cols), jnp.float32),
            pltpu.VMEM((det_rows, REACH * PB // LOW, time_cols), jnp.bfloat16),
            pltpu.VMEM((det_rows, LOW, time_cols), jnp.bfloat16),
            stack,
            pltpu.VMEM((2, SUB, LANE), jnp.float32),
            pltpu.VMEM((REACH, LANE), jnp.float32),
            pltpu.VMEM((REACH, LANE), jnp.float32),
            stack,
            stack,
            stack,
            stack,
            maps,
            maps,
            pltpu.SemaphoreType.DMA((6,)),
            pltpu.SemaphoreType.DMA((6,)),
        ],
        compiler_params=pltpu.CompilerParams(
            collective_id=0, has_side_effects=True, vmem_limit_bytes=64 * 1024 * 1024
        ),
    )(
        block_slot.reshape(1, -1),
        timestreams,
        pointing,
        det_flags.reshape(1, -1),
        det_weight.reshape(1, -1),
        start_modes.T,
    )
    return modes_t.T, signal_map, weight_map


def fits(mesh, timestreams, block_slot, start_modes):
    peers = mesh.shape["det"]
    size = start_modes.shape[1]
    return (
        mesh.shape["tm"] == 1
        and block_slot.shape[0] == peers
        and peers > REACH
        and timestreams.shape[1] * size == peers * SUB * LANE
        and 2 * size == LANE
        and timestreams.shape[0] // (peers * mesh.shape["obs"]) % SUB == 0
    )


def solution(mesh):
    def run(timestreams, pointing, det_flags, det_weight, block_slot, start_modes):
        body = fused_shards if fits(mesh, timestreams, block_slot, start_modes) else shards
        return jax.shard_map(
            body,
            mesh=mesh,
            in_specs=(
                P(("obs", "det"), "tm"),
                P(("obs", "det"), "tm"),
                P(("obs", "det")),
                P(("obs", "det")),
                P(),
                P("tm", None),
            ),
            out_specs=(P(("obs", "tm"), None), P(("obs", "det"), None), P(("obs", "det"), None)),
            check_vma=False,
        )(timestreams, pointing, det_flags, det_weight, block_slot, start_modes)

    return run
```
